512 devices in a mesh: island: 4 (over x_hi, core), fsdp: 128 (over y, z, x_lo).
Axes of the slice: x: 4 (x_hi: 2, x_lo: 2; x = x_hi * 2 + x_lo), y: 4, z: 16, core: 2. Of those that a mesh axis runs over, the one named last changes fastest.
Arguments:
- tokens: bfloat16 [131072, 8192], P(('island', 'fsdp')), may hold values from -24 to 24
- key_grad: bfloat16 [131072, 128], P(('island', 'fsdp')), may hold values from -6 to 6
- weight: float32 [4, 8192, 128], P('island', 'fsdp'), may hold values from -6 to 6
- weight_m: float32 [4, 8192, 128], P('island', 'fsdp'), may hold values from -6 to 6
- weight_v: float32 [4, 8192, 128], P('island', 'fsdp'), may hold values from 0.1 to 10
- gain: float32 [4, 8192], P('island', 'fsdp'), may hold values from 0.1 to 1.9
- gain_m: float32 [4, 8192], P('island', 'fsdp'), may hold values from -24 to 24
- gain_v: float32 [4, 8192], P('island', 'fsdp'), may hold values from 10 to 1000
- outer: float32 [8192, 128], P('fsdp'), may hold values from -6 to 6
- momentum: float32 [8192, 128], P('fsdp'), may hold values from -3 to 3
- fragment_of_row: int32 [8192], P('fsdp'), may hold values from 0 to 3
- active_fragment: int32 [1], replicated, may hold values from 0 to 4095
Outputs:
- keys: bfloat16 [131072, 128], P(('island', 'fsdp'))
- new_weight: float32 [4, 8192, 128], P('island', 'fsdp')
- new_weight_m: float32 [4, 8192, 128], P('island', 'fsdp')
- new_weight_v: float32 [4, 8192, 128], P('island', 'fsdp')
- new_gain: float32 [4, 8192], P('island', 'fsdp')
- new_gain_m: float32 [4, 8192], P('island', 'fsdp')
- new_gain_v: float32 [4, 8192], P('island', 'fsdp')
- new_outer: float32 [8192, 128], P('fsdp')
- new_momentum: float32 [8192, 128], P('fsdp')
The draws below stay inside these ranges and needn't reach their ends.
Inputs may be any that keep to these rules, and one draw needn't show every extreme that they name: `active_fragment`: an outer step number, zero or more.
All inputs are finite; a program needn't handle non-finite values.
Results may differ from the reference program's by a relative error of at most 0.009.
Values may be sent and summed in bfloat16 or wider, within the bound.
A program may use at most 128 MiB of HBM per device.

```python
import math
import jax
import jax.numpy as jnp
from jax import lax

D = 8192
HD = 128
NFRAG = 4
TOK_DEV = 256
TOKENS = 131072
N_ISLAND = 4
N_FSDP = 128


def touch_ends(drawn, stream_key, smallest, largest):
    longest = drawn.shape.index(max(drawn.shape))
    spots = []
    for shift in (0, 1):
        where = [jax.random.randint(jax.random.fold_in(stream_key, axis), (), 0, length) for axis, length in enumerate(drawn.shape)]
        where[longest] = (where[longest] + shift) % drawn.shape[longest]
        spots.append(tuple(where))
    return drawn.at[spots[0]].set(smallest).at[spots[1]].set(largest)


def strengthened(drawn, key, source, target, shards_of, factor):
    def block_of(position):
        return (jnp.arange(drawn.shape[position]) // (drawn.shape[position] // shards_of)).reshape((-1,) + (1,) * (drawn.ndim - 1 - position))

    first = jax.random.permutation(key, shards_of)[block_of(target)]
    second = (block_of(target) + shards_of // 2) % shards_of
    return jnp.where((block_of(source) == first) | (block_of(source) == second), factor * drawn, drawn)


def levels(key, dims, pieces, least, largest):
    loudness, own = 1.0, jax.random.fold_in(key, 6)
    for dim, shards_of in pieces:
        heights = jnp.exp(jax.random.uniform(jax.random.fold_in(own, dim), (shards_of,), jnp.float32, least / len(pieces), largest / len(pieces)))
        loudness = loudness * jnp.repeat(heights, dims[dim] // shards_of).reshape([-1 if axis == dim else 1 for axis in range(len(dims))])
    return loudness


def centred(rng, dims, scale, reach, pieces=(), dtype=jnp.bfloat16):
    factor_of = levels(rng, dims, pieces, -0.22, 0.18) if pieces else 1.0
    result = jax.random.normal(rng, dims, jnp.float32) * scale * factor_of
    return jnp.minimum(jnp.maximum(result, -reach), reach).astype(dtype)


def bell_draw_with(own_key, shape, spread, bound, pieces, heavy, dtype=jnp.bfloat16):
    drawn = spread * jax.random.normal(own_key, shape, jnp.float32)
    if pieces:
        drawn = drawn * levels(own_key, shape, pieces, -0.22, 0.18)
    return jnp.clip(strengthened(drawn, jax.random.fold_in(own_key, 3), *heavy), -bound, bound).astype(dtype)


def setup_inputs(seed: int = 0) -> dict:
    keys = jax.random.split(jax.random.key(seed), 13)
    return {
        "tokens": bell_draw_with(keys[0], (TOKENS, D), 1.0, 24.0, ((0, 512),), (0, 1, 512, 6.0)),
        "key_grad": centred(keys[1], (TOKENS, HD), 1.0, 6.0, ((0, 512),)),
        "weight": centred(keys[2], (N_ISLAND, D, HD), 1.0, 6.0, ((0, 4), (1, 128)), jnp.float32),
        "weight_m": centred(keys[3], (N_ISLAND, D, HD), 1.0, 6.0, ((0, 4), (1, 128)), jnp.float32),
        "weight_v": jnp.clip(jnp.exp(math.log(10.0) - 4.6051702 * jax.random.uniform(keys[4], (N_ISLAND, D, HD), jnp.float32) ** levels(keys[4], (N_ISLAND, D, HD), ((0, 4), (1, 128)), -0.2, 0.2)), 0.1, 10.0),
        "gain": jnp.clip(1.0 + 0.18 * jax.random.normal(keys[5], (N_ISLAND, D), jnp.float32), 0.1, 1.9),
        "gain_m": centred(keys[6], (N_ISLAND, D), 4.0, 24.0, ((0, 4), (1, 128)), jnp.float32),
        "gain_v": jnp.clip(jnp.exp(math.log(1000.0) - 4.6051702 * jax.random.uniform(keys[7], (N_ISLAND, D), jnp.float32) ** levels(keys[7], (N_ISLAND, D), ((0, 4), (1, 128)), -0.2, 0.2)), 10.0, 1000.0),
        "outer": centred(keys[8], (D, HD), 1.0, 6.0, ((0, 128),), jnp.float32),
        "momentum": centred(keys[9], (D, HD), 0.5, 3.0, ((0, 128),), jnp.float32),
        "fragment_of_row": touch_ends(jax.random.randint(keys[10], (D,), 0, NFRAG), jax.random.fold_in(keys[10], 1), 0, NFRAG - 1).astype(jnp.int32),
        "active_fragment": jax.random.randint(keys[11], (1,), 0, NFRAG * 1024).astype(jnp.int32),
    }


NORM_EPS = 1e-05
BETA_ONE = 0.9
BETA_TWO = 0.999
ADAM_EPS = 1e-08
INNER_LR = 0.01
DECAY = 0.1
OUTER_LR = 0.7
OUTER_MU = 0.9
MIX_KEEP = 0.5

def adam_step(param, grad, first, second):
    first = BETA_ONE * first + (1.0 - BETA_ONE) * grad
    second = BETA_TWO * second + (1.0 - BETA_TWO) * grad * grad
    param = param - INNER_LR * (first / (jnp.sqrt(second) + ADAM_EPS) + DECAY * param)
    return (param, first, second)

def reference(tokens, key_grad, weight, weight_m, weight_v, gain, gain_m, gain_v, outer, momentum, fragment_of_row, active_fragment):
    key_scale = D ** (-0.5)
    per_island = TOK_DEV * N_FSDP
    outer_drift = lax.optimization_barrier(jnp.sum(outer[None] - weight, axis=0)) / N_ISLAND
    pushed = OUTER_MU * momentum + outer_drift
    candidate = outer - OUTER_LR * (OUTER_MU * pushed + outer_drift)
    current = active_fragment[0] % NFRAG
    in_fragment = (fragment_of_row == current)[:, None]
    new_momentum = jnp.where(in_fragment, pushed, momentum)
    new_outer = jnp.where(in_fragment, candidate, outer)
    key_parts, weight_list, wm_list, wv_list, gain_list, gm_list, gv_list = ([], [], [], [], [], [], [])
    for island_index in range(N_ISLAND):
        values = tokens[island_index * per_island:(island_index + 1) * per_island].astype(jnp.float32)
        cotangent = key_grad[island_index * per_island:(island_index + 1) * per_island]
        root_mean = jnp.sqrt(lax.optimization_barrier(jnp.mean(values * values, axis=1)) + NORM_EPS)
        unit_rows = values / root_mean[:, None]
        gain_bf = lax.optimization_barrier(gain[island_index].astype(jnp.bfloat16))
        weight_bf = weight[island_index].astype(jnp.bfloat16)
        normed = (unit_rows * gain_bf.astype(jnp.float32)).astype(jnp.bfloat16)
        key_parts.append((key_scale * jnp.dot(normed, weight_bf, preferred_element_type=jnp.float32)).astype(jnp.bfloat16))
        weight_grad = key_scale * jnp.dot(normed.T, cotangent, preferred_element_type=jnp.float32)
        back_grad = key_scale * jnp.dot(cotangent, weight_bf.T, preferred_element_type=jnp.float32)
        gain_grad = lax.optimization_barrier(jnp.sum(back_grad * unit_rows, axis=0))
        inner, first, second = adam_step(weight[island_index], weight_grad, weight_m[island_index], weight_v[island_index])
        gain_new, gain_first, gain_second = adam_step(gain[island_index], gain_grad, gain_m[island_index], gain_v[island_index])
        weight_list.append(jnp.where(in_fragment, MIX_KEEP * inner + (1.0 - MIX_KEEP) * candidate, inner))
        wm_list.append(first)
        wv_list.append(second)
        gain_list.append(gain_new)
        gm_list.append(gain_first)
        gv_list.append(gain_second)
    return (jnp.concatenate(key_parts, axis=0), jnp.stack(weight_list), jnp.stack(wm_list), jnp.stack(wv_list), jnp.stack(gain_list), jnp.stack(gm_list), jnp.stack(gv_list), new_outer, new_momentum)
```

```python
import jax
import jax.numpy as jnp
from jax import lax
from jax.experimental import pallas as pl
from jax.experimental.pallas import tpu as pltpu
from jax.sharding import PartitionSpec as P

NFRAG = 4
NORM_EPS = 1e-05
BETA_ONE = 0.9
BETA_TWO = 0.999
ADAM_EPS = 1e-08
INNER_LR = 0.01
DECAY = 0.1
OUTER_LR = 0.7
OUTER_MU = 0.9
MIX_KEEP = 0.5

MESH = pl.DeviceIdType.MESH
NY, NZ, NX, NI = 4, 16, 2, 4
TOK, WIDTH, HEAD = 256, 8192, 128
ROWS = 64
BLOCK = NX * ROWS
YSTEP = (0, 1, 3, 2)
F32, BF16 = jnp.float32, jnp.bfloat16


def exchange(
    x_hbm,
    kg,
    weight,
    gain,
    outer,
    keys_out,
    usum_out,
    drift_out,
    xv,
    gw,
    part,
    s_a,
    r_a,
    s_bp,
    s_bm,
    r_bp,
    r_bm,
    s_zp,
    s_zm,
    r_zp,
    r_zm,
    own,
    total,
    r_x,
    diffs,
    acc,
    kgt,
    inv,
    sem_x,
    gz_recv,
    gx_recv,
    gy_recv,
    g_send,
    a_recv,
    b_recv,
    z_recv,
    rs_send,
    tail_send,
    tail_recv,
    d_send,
    d_recv,
):
    isl, f = lax.axis_index("island"), lax.axis_index("fsdp")
    y, z, xl = f // (NZ * NX), (f // NX) % NZ, f % NX

    def device(dy=0, dz=0, flip=False):
        yy, zz = (y + NY + dy) % NY, (z + NZ + dz) % NZ
        xx = 1 - xl if flip else xl
        return (isl, (yy * NZ + zz) * NX + xx)

    up_y, down_y, up_z, down_z = device(dy=1), device(dy=-1), device(dz=1), device(dz=-1)
    partner = device(flip=True)
    islands = [((isl + k) % NI, f) for k in range(1, NI)]

    barrier = pltpu.get_barrier_semaphore()
    peers = [up_y, down_y, up_z, down_z, partner] + islands
    for peer in peers:
        pl.semaphore_signal(barrier, inc=1, device_id=peer, device_id_type=MESH)

    def load(n, carry):
        for c in range(2):
            r = 8 - n if c == 0 else (8 + n + 8 * ((8 - n) // 8)) % NZ
            for p in range(NY):
                block = ((y + YSTEP[p]) % NY) * NZ + (z + r) % NZ
                pltpu.make_async_copy(
                    x_hbm.at[:, pl.ds(pl.multiple_of(block * BLOCK, BLOCK), BLOCK)],
                    xv.at[n, :, pl.ds((c * NY + p) * BLOCK, BLOCK)],
                    sem_x.at[n],
                ).start()
        return carry

    lax.fori_loop(0, 8, load, 0)

    def remote(src, dst, send, recv, to):
        return pltpu.make_async_remote_copy(
            src_ref=src,
            dst_ref=dst,
            send_sem=send,
            recv_sem=recv,
            device_id=to,
            device_id_type=MESH,
        )

    def await_recv(ref, sem):
        pltpu.make_async_copy(ref, ref, sem).wait()

    half = pl.ds(pl.multiple_of(xl * ROWS, ROWS), ROWS)
    other = pl.ds(pl.multiple_of((1 - xl) * ROWS, ROWS), ROWS)
    low = pl.ds(pl.multiple_of(xl * ROWS, ROWS), ROWS // 2)
    high = pl.ds(pl.multiple_of(xl * ROWS + ROWS // 2, ROWS // 2), ROWS // 2)

    eye = lax.broadcasted_iota(jnp.int32, (ROWS, ROWS), 0) == lax.broadcasted_iota(
        jnp.int32, (ROWS, ROWS), 1
    )
    gain_bf = gain[...].astype(BF16).astype(F32)
    column = jnp.sum(jnp.where(eye, gain_bf, 0.0), axis=1, keepdims=True)
    w = weight[0]
    gw[1, 0, half, :] = (column * w.astype(BF16).astype(F32)).astype(BF16)
    diffs[isl] = (outer[...] - w).astype(BF16)

    pl.semaphore_wait(barrier, len(peers))

    mine = gw.at[1, 0, half]
    remote(mine, mine, g_send.at[0], gx_recv.at[16], partner).start()
    remote(mine, gw.at[1, 2, half], g_send.at[1], gy_recv.at[2], up_y).start()
    remote(mine, gw.at[1, 1, half], g_send.at[2], gy_recv.at[1], down_y).start()
    for k in range(1, NI):
        remote(
            diffs.at[isl], diffs.at[isl], d_send.at[k], d_recv.at[NI - k], islands[k - 1]
        ).start()

    def rows(p):
        return pl.ds(0, BLOCK) if p == 0 else half

    def send_z(p, c, src, dst):
        to = down_z if c == 0 else up_z
        remote(
            gw.at[src, p, rows(p)],
            gw.at[dst, p, rows(p)],
            g_send.at[3 if p == 0 else 4],
            gz_recv.at[dst, p],
            to,
        ).start()

    def wait_z(p, n, c):
        await_recv(gw.at[2 * n + c, p, rows(p)], gz_recv.at[2 * n + c, p])

    def send_x(n, c):
        block = gw.at[2 * n + c, pl.ds(1, 3), half]
        remote(block, block, g_send.at[5], gx_recv.at[2 * n + c], partner).start()

    def wait_x(n, c):
        await_recv(gw.at[2 * n + c, pl.ds(1, 3), other], gx_recv.at[2 * n + c])

    def squares(n, carry):
        await_recv(xv.at[n], sem_x.at[n])
        for k in range(2 * NY):
            v = xv[n, :, k * BLOCK : (k + 1) * BLOCK].astype(F32)
            inv[...] += v * v
        return carry

    inv[...] = jnp.zeros_like(inv)
    acc[...] = jnp.zeros_like(acc)
    lax.fori_loop(0, 4, squares, 0)
    await_recv(gw.at[1, 0, other], gx_recv.at[16])
    for c in range(2):
        send_z(0, c, 1, 14 + c)
    await_recv(gw.at[1, 2, half], gy_recv.at[2])
    remote(gw.at[1, 2, low], gw.at[1, 3, low], g_send.at[6], gy_recv.at[3], up_y).start()
    await_recv(gw.at[1, 1, half], gy_recv.at[1])
    remote(gw.at[1, 1, high], gw.at[1, 3, high], g_send.at[7], gy_recv.at[4], down_y).start()
    for p in (1, 2):
        for c in range(2):
            send_z(p, c, 1, 14 + c)
    lax.fori_loop(4, 8, squares, 0)
    scale = lax.rsqrt(jnp.sum(inv[...], axis=1, keepdims=True) * (1.0 / WIDTH) + NORM_EPS)
    inv[...] = jnp.broadcast_to(scale, inv.shape)
    kgt[...] = (kg[...].astype(F32) * inv[...]).T.astype(BF16)

    def block_of(n, c, p):
        lanes = (c * NY + p) * BLOCK
        return part[n, :, lanes : lanes + BLOCK]

    def step_one(n):
        part[n] = jnp.dot(kgt[...], xv[n], preferred_element_type=F32)
        for c in range(2):
            s_a[n, c] = block_of(n, c, 3).astype(BF16)
        top, bottom = pl.ds(0, HEAD // 2), pl.ds(HEAD // 2, HEAD // 2)
        remote(
            s_a.at[n, :, top], r_a.at[n, :, top], rs_send.at[0], a_recv.at[n, 0], up_y
        ).start()
        remote(
            s_a.at[n, :, bottom], r_a.at[n, :, bottom], rs_send.at[0], a_recv.at[n, 1], down_y
        ).start()

    def step_two(n):
        h = HEAD // 2
        await_recv(r_a.at[n, :, pl.ds(0, h)], a_recv.at[n, 0])
        for c in range(2):
            mine = block_of(n, c, 1)
            s_bp[n, c, :h] = (mine[:h] + r_a[n, c, :h].astype(F32)).astype(BF16)
            s_bp[n, c, h:] = mine[h:].astype(BF16)
        remote(s_bp.at[n], r_bp.at[n], rs_send.at[1], b_recv.at[n, 0], up_y).start()
        await_recv(r_a.at[n, :, pl.ds(h, h)], a_recv.at[n, 1])
        for c in range(2):
            mine = block_of(n, c, 2)
            s_bm[n, c, :h] = mine[:h].astype(BF16)
            s_bm[n, c, h:] = (mine[h:] + r_a[n, c, h:].astype(F32)).astype(BF16)
        remote(s_bm.at[n], r_bm.at[n], rs_send.at[2], b_recv.at[n, 1], down_y).start()

    r_zp[0] = jnp.zeros((HEAD, BLOCK), BF16)
    r_zm[0] = jnp.zeros((HEAD, BLOCK), BF16)
    r_zm[1] = jnp.zeros((HEAD, BLOCK), BF16)

    def step_three(n):
        await_recv(r_bp.at[n], b_recv.at[n, 0])
        await_recv(r_bm.at[n], b_recv.at[n, 1])
        sums = [
            block_of(n, c, 0) + r_bp[n, c].astype(F32) + r_bm[n, c].astype(F32) for c in range(2)
        ]

        @pl.when(n >= 1)
        def _():
            await_recv(r_zp.at[n], z_recv.at[n, 0])

        s_zp[n] = (sums[0] + r_zp[n].astype(F32)).astype(BF16)
        remote(s_zp.at[n], r_zp.at[n + 1], rs_send.at[3], z_recv.at[n + 1, 0], up_z).start()

        @pl.when(n == 0)
        def _():
            own[...] = sums[1]

        @pl.when(n >= 2)
        def _():
            await_recv(r_zm.at[n], z_recv.at[n, 1])

        @pl.when(n >= 1)
        def _():
            s_zm[n] = (sums[1] + r_zm[n].astype(F32)).astype(BF16)
            remote(
                s_zm.at[n], r_zm.at[n + 1], rs_send.at[4], z_recv.at[n + 1, 1], down_z
            ).start()

    def keys_part(n):
        for c in range(2):
            wait_x(n, c)
        acc[...] += jnp.dot(
            xv[n], gw[pl.ds(2 * n, 2)].reshape(2 * NY * BLOCK, HEAD), preferred_element_type=F32
        )

    step_one(0)
    await_recv(gw.at[1, 3, low], gy_recv.at[3])
    await_recv(gw.at[1, 3, high], gy_recv.at[4])
    for c in range(2):
        send_z(3, c, 1, 14 + c)
    send_x(0, 1)

    def iteration(i, carry):
        @pl.when(i <= 6)
        def _():
            n = 8 - i
            for p in range(NY):
                for c in range(2):
                    wait_z(p, n, c)
                    send_z(p, c, 2 * n + c, 2 * n - 2 + c)
            for c in range(2):
                send_x(n, c)

        @pl.when(i == 7)
        def _():
            for p in range(NY):
                for c in range(2):
                    wait_z(p, 1, c)
                    if c == (1 if p < 2 else 0):
                        send_z(p, c, 2 + c, 0)
            for c in range(2):
                send_x(1, c)

        @pl.when(i == 8)
        def _():
            for p in range(NY):
                wait_z(p, 0, 0)
            send_x(0, 0)

        @pl.when(i <= 7)
        def _():
            step_one(i)

        @pl.when(i <= 8)
        def _():
            step_two(i - 1)

        @pl.when(i >= 2)
        def _():
            step_three(i - 2)
            keys_part(9 - i)

        return carry

    lax.fori_loop(1, 10, iteration, 0)

    await_recv(r_zp.at[8], z_recv.at[8, 0])
    await_recv(r_zm.at[8], z_recv.at[8, 1])
    total[...] = (own[...] + r_zp[8].astype(F32) + r_zm[8].astype(F32)).T
    remote(total.at[other], r_x, tail_send, tail_recv, partner).start()

    keys_out[...] = (acc[...] * (inv[...] * WIDTH ** (-0.5))).astype(BF16)
    for k in range(1, NI):
        await_recv(diffs.at[(isl + k) % NI], d_recv.at[k])
    summed = diffs[0].astype(F32)
    for k in range(1, NI):
        summed = summed + diffs[k].astype(F32)
    drift_out[...] = summed * (1.0 / NI)

    for k in (0, 1, 2):
        await_recv(mine, g_send.at[k])
    await_recv(gw.at[pl.ds(1, 15), 0], g_send.at[3])
    await_recv(gw.at[pl.ds(1, 15), pl.ds(1, 3), half], g_send.at[4])
    await_recv(gw.at[:, pl.ds(1, 3), half], g_send.at[5])
    await_recv(gw.at[1, 3, low], g_send.at[6])
    await_recv(gw.at[1, 3, high], g_send.at[7])
    for k in range(1, NI):
        await_recv(diffs.at[0], d_send.at[k])
    await_recv(s_a, rs_send.at[0])
    await_recv(s_bp, rs_send.at[1])
    await_recv(s_bm, rs_send.at[2])
    await_recv(s_zp, rs_send.at[3])
    await_recv(s_zm.at[pl.ds(1, 7)], rs_send.at[4])
    await_recv(total.at[other], tail_send)

    await_recv(r_x, tail_recv)
    usum_out[...] = total[half, :] + r_x[...]


def adam_step(param, grad, first, second):
    first = BETA_ONE * first + (1.0 - BETA_ONE) * grad
    second = BETA_TWO * second + (1.0 - BETA_TWO) * grad * grad
    param = param - INNER_LR * (first / (jnp.sqrt(second) + ADAM_EPS) + DECAY * param)
    return (param, first, second)


def shards(
    tokens,
    key_grad,
    weight,
    weight_m,
    weight_v,
    gain,
    gain_m,
    gain_v,
    outer,
    momentum,
    fragment_of_row,
    active_fragment,
):
    vmem = pl.BlockSpec(memory_space=pltpu.VMEM)
    block = (HEAD, BLOCK)
    dma = pltpu.SemaphoreType.DMA
    keys, unit_sum, outer_drift = pl.pallas_call(
        exchange,
        out_shape=(
            jax.ShapeDtypeStruct((TOK, HEAD), BF16),
            jax.ShapeDtypeStruct((ROWS, HEAD), F32),
            jax.ShapeDtypeStruct((ROWS, HEAD), F32),
        ),
        in_specs=[pl.BlockSpec(memory_space=pl.ANY)] + [vmem] * 4,
        out_specs=(vmem, vmem, vmem),
        scratch_shapes=[
            pltpu.VMEM((8, TOK, 2 * NY * BLOCK), BF16),
            pltpu.VMEM((NZ, NY, BLOCK, HEAD), BF16),
            pltpu.VMEM((8, HEAD, 2 * NY * BLOCK), F32),
            pltpu.VMEM((8, 2) + block, BF16),
            pltpu.VMEM((8, 2) + block, BF16),
            pltpu.VMEM((8, 2) + block, BF16),
            pltpu.VMEM((8, 2) + block, BF16),
            pltpu.VMEM((8, 2) + block, BF16),
            pltpu.VMEM((8, 2) + block, BF16),
            pltpu.VMEM((8,) + block, BF16),
            pltpu.VMEM((8,) + block, BF16),
            pltpu.VMEM((9,) + block, BF16),
            pltpu.VMEM((9,) + block, BF16),
            pltpu.VMEM(block, F32),
            pltpu.VMEM(block, F32),
            pltpu.VMEM((ROWS, HEAD), F32),
            pltpu.VMEM((NI, ROWS, HEAD), BF16),
            pltpu.VMEM((TOK, HEAD), F32),
            pltpu.VMEM((HEAD, TOK), BF16),
            pltpu.VMEM((TOK, HEAD), F32),
            dma((8,)),
            dma((NZ, NY)),
            dma((NZ + 1,)),
            dma((5,)),
            dma((8,)),
            dma((8, 2)),
            dma((8, 2)),
            dma((9, 2)),
            dma((5,)),
            dma,
            dma,
            dma((NI,)),
            dma((NI,)),
        ],
        compiler_params=pltpu.CompilerParams(
            collective_id=0, has_side_effects=True, vmem_limit_bytes=40 * 2**20
        ),
        cost_estimate=pl.CostEstimate(
            flops=4 * TOK * WIDTH * HEAD, bytes_accessed=2 * TOK * WIDTH, transcendentals=0
        ),
    )(tokens, key_grad, weight, gain, outer)
    key_scale = WIDTH ** (-0.5)
    weight_bf = weight[0].astype(BF16).astype(F32)
    gain_bf = gain[0].astype(BF16).astype(F32)
    weight_grad = key_scale * gain_bf[:, None] * unit_sum
    gain_grad = key_scale * jnp.sum(weight_bf * unit_sum, axis=1)
    inner, first, second = adam_step(weight[0], weight_grad, weight_m[0], weight_v[0])
    gain_new, gain_first, gain_second = adam_step(gain[0], gain_grad, gain_m[0], gain_v[0])
    pushed = OUTER_MU * momentum + outer_drift
    candidate = outer - OUTER_LR * (OUTER_MU * pushed + outer_drift)
    current = active_fragment[0] % NFRAG
    in_fragment = (fragment_of_row == current)[:, None]
    new_momentum = jnp.where(in_fragment, pushed, momentum)
    new_outer = jnp.where(in_fragment, candidate, outer)
    merged = jnp.where(in_fragment, MIX_KEEP * inner + (1.0 - MIX_KEEP) * candidate, inner)
    return (
        keys,
        merged[None],
        first[None],
        second[None],
        gain_new[None],
        gain_first[None],
        gain_second[None],
        new_outer,
        new_momentum,
    )


def solution(mesh):
    return jax.shard_map(
        shards,
        mesh=mesh,
        in_specs=(
            P(("island", "fsdp"), None),
            P(("island", "fsdp"), None),
            P("island", "fsdp", None),
            P("island", "fsdp", None),
            P("island", "fsdp", None),
            P("island", "fsdp"),
            P("island", "fsdp"),
            P("island", "fsdp"),
            P("fsdp", None),
            P("fsdp", None),
            P("fsdp"),
            P(),
        ),
        out_specs=(
            P(("island", "fsdp"), None),
            P("island", "fsdp", None),
            P("island", "fsdp", None),
            P("island", "fsdp", None),
            P("island", "fsdp"),
            P("island", "fsdp"),
            P("island", "fsdp"),
            P("fsdp", None),
            P("fsdp", None),
        ),
        check_vma=False,
    )
```

```python
import jax
import jax.numpy as jnp
from jax import lax
from jax.experimental import pallas as pl
from jax.experimental.pallas import tpu as pltpu
from jax.sharding import PartitionSpec as P

NFRAG = 4
NORM_EPS = 1e-05
BETA_ONE = 0.9
BETA_TWO = 0.999
ADAM_EPS = 1e-08
INNER_LR = 0.01
DECAY = 0.1
OUTER_LR = 0.7
OUTER_MU = 0.9
MIX_KEEP = 0.5

MESH = pl.DeviceIdType.MESH
NY, NZ, NX, NI = 4, 16, 2, 4
TOK, WIDTH, HEAD = 256, 8192, 128
ROWS = 64
BLOCK = NX * ROWS
ZSTEP = (0, 1, -2, -1)
ORDER = (2, 1, 3, 0)
GROUP = NY * 4 * BLOCK
F32, BF16 = jnp.float32, jnp.bfloat16


def exchange(
    x_hbm,
    kg_hbm,
    weight_hbm,
    gain_hbm,
    outer_hbm,
    keys_out,
    usum_out,
    drift_out,
    xv,
    gw,
    part,
    s_a,
    r_a,
    s_bp,
    s_bm,
    r_bp,
    r_bm,
    s_z,
    r_z,
    s_h,
    r_h,
    own,
    total,
    r_x,
    diffs,
    acc,
    kgt,
    inv,
    kg,
    weight,
    gain,
    outer,
    sem_in,
    sem_x,
    gh_recv,
    gz_recv,
    gy_recv,
    gx_recv,
    g_send,
    a_recv,
    b_recv,
    z_recv,
    h_recv,
    rs_send,
    tail_send,
    tail_recv,
    d_send,
    d_recv,
):
    isl, f = lax.axis_index("island"), lax.axis_index("fsdp")
    y, z, xl = f // (NZ * NX), (f // NX) % NZ, f % NX

    def device(dy=0, dz=0, flip=False):
        yy, zz = (y + NY + dy) % NY, (z + NZ + dz) % NZ
        xx = 1 - xl if flip else xl
        return (isl, (yy * NZ + zz) * NX + xx)

    loads = [
        pltpu.make_async_copy(src, dst, sem_in.at[k])
        for k, (src, dst) in enumerate(
            [(weight_hbm, weight), (gain_hbm, gain), (outer_hbm, outer), (kg_hbm, kg)]
        )
    ]
    for copy in loads:
        copy.start()
    up_y, down_y = device(dy=1), device(dy=-1)
    near = {d: device(dz=d) for d in (1, -1, 2, -2)}
    far = {k: device(dz=d) for k, d in ((1, 4), (2, 8), (3, -4))}
    partner = device(flip=True)
    islands = [((isl + k) % NI, f) for k in range(1, NI)]

    barrier = pltpu.get_barrier_semaphore()
    peers = [up_y, down_y, partner] + list(near.values()) + list(far.values()) + islands
    for peer in peers:
        pl.semaphore_signal(barrier, inc=1, device_id=peer, device_id_type=MESH)

    def load(k):
        def one(q, carry):
            for j in range(4):
                block = ((y + q) % NY) * NZ + (z + NZ + 4 * k + ZSTEP[j]) % NZ
                pltpu.make_async_copy(
                    x_hbm.at[:, pl.ds(pl.multiple_of(block * BLOCK, BLOCK), BLOCK)],
                    xv.at[k, :, pl.ds(pl.multiple_of((q * 4 + j) * BLOCK, BLOCK), BLOCK)],
                    sem_x.at[k],
                ).start()
            return carry

        lax.fori_loop(0, NY, one, 0)

    for k in ORDER:
        load(k)

    def remote(src, dst, send, recv, to):
        return pltpu.make_async_remote_copy(
            src_ref=src,
            dst_ref=dst,
            send_sem=send,
            recv_sem=recv,
            device_id=to,
            device_id_type=MESH,
        )

    def await_recv(ref, sem):
        pltpu.make_async_copy(ref, ref, sem).wait()

    half = pl.ds(pl.multiple_of(xl * ROWS, ROWS), ROWS)
    other = pl.ds(pl.multiple_of((1 - xl) * ROWS, ROWS), ROWS)
    first, last = pl.ds(0, 2), pl.ds(2, 2)

    for copy in loads[:3]:
        copy.wait()
    eye = lax.broadcasted_iota(jnp.int32, (ROWS, ROWS), 0) == lax.broadcasted_iota(
        jnp.int32, (ROWS, ROWS), 1
    )
    gain_bf = gain[...].astype(BF16).astype(F32)
    column = jnp.sum(jnp.where(eye, gain_bf, 0.0), axis=1, keepdims=True)
    w = weight[0]
    gw[0, 0, 0, half, :] = (column * w.astype(BF16).astype(F32)).astype(BF16)
    diffs[isl] = (outer[...] - w).astype(BF16)

    def send_far(k):
        remote(
            gw.at[0, 0, 0, half], gw.at[4 - k, 0, 0, half], g_send.at[0], gh_recv.at[4 - k], far[k]
        ).start()

    def wait_far(k):
        await_recv(gw.at[k, 0, 0, half], gh_recv.at[k])

    def send_near(k):
        for j, d in ((2, 2), (3, 1), (1, -1)):
            remote(
                gw.at[k, 0, 0, half], gw.at[k, 0, j, half], g_send.at[1], gz_recv.at[k, j], near[d]
            ).start()

    def send_x(k, q):
        block = gw.at[k, q, :, half]
        remote(block, block, g_send.at[4], gx_recv.at[k, q], partner).start()

    def send_y(k):
        for j in (1, 3, 2):
            await_recv(gw.at[k, 0, j, half], gz_recv.at[k, j])
        block = gw.at[k, 0, :, half]
        remote(block, gw.at[k, 3, :, half], g_send.at[2], gy_recv.at[k, 3], up_y).start()
        remote(block, gw.at[k, 1, :, half], g_send.at[2], gy_recv.at[k, 1], down_y).start()
        send_x(k, 0)

    def forward_y(k):
        await_recv(gw.at[k, 3, :, half], gy_recv.at[k, 3])
        remote(
            gw.at[k, 3, first, half], gw.at[k, 2, first, half], g_send.at[3], gy_recv.at[k, 0], up_y
        ).start()
        await_recv(gw.at[k, 1, :, half], gy_recv.at[k, 1])
        remote(
            gw.at[k, 1, last, half], gw.at[k, 2, last, half], g_send.at[3], gy_recv.at[k, 2], down_y
        ).start()
        send_x(k, 3)
        send_x(k, 1)

    def opposite(k):
        await_recv(gw.at[k, 2, first, half], gy_recv.at[k, 0])
        await_recv(gw.at[k, 2, last, half], gy_recv.at[k, 2])
        send_x(k, 2)

    def keys_part(k, q):
        await_recv(gw.at[k, q, :, other], gx_recv.at[k, q])
        columns = pl.ds(q * 4 * BLOCK, 4 * BLOCK)
        acc[...] += jnp.dot(
            xv[k, :, columns], gw[k, q].reshape(4 * BLOCK, HEAD), preferred_element_type=F32
        )

    def block_of(k, q, j):
        lanes = (q * 4 + j) * BLOCK
        return part[k, :, lanes : lanes + BLOCK]

    def step_one(k):
        part[k] = jnp.dot(kgt[...], xv[k], preferred_element_type=F32)
        for j in range(4):
            s_a[k, j] = block_of(k, 2, j).astype(BF16)
        remote(s_a.at[k, first], r_a.at[k, first], rs_send.at[0], a_recv.at[k, 0], up_y).start()
        remote(s_a.at[k, last], r_a.at[k, last], rs_send.at[0], a_recv.at[k, 1], down_y).start()

    def step_two(k):
        await_recv(r_a.at[k, first], a_recv.at[k, 0])
        for j in range(4):
            mine = block_of(k, 1, j)
            s_bp[k, j] = (mine + r_a[k, j].astype(F32) if j < 2 else mine).astype(BF16)
        remote(s_bp.at[k], r_bp.at[k], rs_send.at[1], b_recv.at[k, 0], up_y).start()
        await_recv(r_a.at[k, last], a_recv.at[k, 1])
        for j in range(4):
            mine = block_of(k, 3, j)
            s_bm[k, j] = (mine if j < 2 else mine + r_a[k, j].astype(F32)).astype(BF16)
        remote(s_bm.at[k], r_bm.at[k], rs_send.at[2], b_recv.at[k, 1], down_y).start()

    def step_three(k):
        await_recv(r_bp.at[k], b_recv.at[k, 0])
        await_recv(r_bm.at[k], b_recv.at[k, 1])
        for j in (2, 1, 3, 0):
            summed = block_of(k, 0, j) + r_bp[k, j].astype(F32) + r_bm[k, j].astype(F32)
            if j == 0:
                own[k] = summed
            else:
                s_z[k, j - 1] = summed.astype(BF16)
                remote(
                    s_z.at[k, j - 1],
                    r_z.at[k, j - 1],
                    rs_send.at[3],
                    z_recv.at[k, j - 1],
                    near[ZSTEP[j]],
                ).start()

    def step_four(k):
        summed = own[k]
        for j in range(3):
            await_recv(r_z.at[k, j], z_recv.at[k, j])
            summed = summed + r_z[k, j].astype(F32)
        if k == 0:
            own[0] = summed
        else:
            s_h[k] = summed.astype(BF16)
            remote(s_h.at[k], r_h.at[k], rs_send.at[4], h_recv.at[k], far[k]).start()

    inv[...] = jnp.zeros_like(inv)
    acc[...] = jnp.zeros_like(acc)
    for k in ORDER:
        await_recv(xv.at[k], sem_x.at[k])

        def squares(q, carry):
            for j in range(4):
                lanes = pl.ds(pl.multiple_of((q * 4 + j) * BLOCK, BLOCK), BLOCK)
                v = xv[k, :, lanes].astype(F32)
                inv[...] += v * v
            return carry

        lax.fori_loop(0, NY, squares, 0)
    scale = lax.rsqrt(jnp.sum(inv[...], axis=1, keepdims=True) * (1.0 / WIDTH) + NORM_EPS)
    inv[...] = jnp.broadcast_to(scale, inv.shape)
    loads[3].wait()
    kgt[...] = (kg[...].astype(F32) * inv[...]).T.astype(BF16)

    pl.semaphore_wait(barrier, len(peers))
    for k in (2, 1, 3):
        send_far(k)
    send_near(0)
    for k in range(1, NI):
        remote(
            diffs.at[isl], diffs.at[isl], d_send.at[k], d_recv.at[NI - k], islands[k - 1]
        ).start()

    for k in ORDER:
        step_one(k)
    send_y(0)
    wait_far(1)
    send_near(1)
    wait_far(3)
    send_near(3)
    step_two(2)
    wait_far(2)
    send_near(2)
    step_two(1)
    send_y(1)
    step_two(3)
    step_two(0)
    forward_y(0)
    send_y(3)
    step_three(2)
    forward_y(1)
    keys_part(0, 0)
    step_three(1)
    send_y(2)
    step_four(2)
    opposite(0)
    keys_part(1, 0)
    forward_y(3)
    step_three(3)
    keys_part(3, 0)
    opposite(1)
    step_four(1)
    step_three(0)
    forward_y(2)
    keys_part(2, 0)
    keys_part(0, 3)
    keys_part(0, 1)
    opposite(3)
    keys_part(1, 3)
    keys_part(1, 1)
    step_four(3)
    opposite(2)
    keys_part(3, 3)
    keys_part(3, 1)
    step_four(0)
    keys_part(2, 3)
    keys_part(2, 1)
    keys_part(0, 2)
    keys_part(1, 2)

    for k in (1, 2, 3):
        await_recv(r_h.at[k], h_recv.at[k])
    total[...] = (
        own[0] + r_h[1].astype(F32) + r_h[2].astype(F32) + r_h[3].astype(F32)
    ).T
    remote(total.at[other], r_x, tail_send, tail_recv, partner).start()

    for k in (3, 2):
        keys_part(k, 2)
    keys_out[...] = acc[...] * (inv[...] * WIDTH ** (-0.5))
    for k in range(1, NI):
        await_recv(diffs.at[(isl + k) % NI], d_recv.at[k])
    summed = diffs[0].astype(F32)
    for k in range(1, NI):
        summed = summed + diffs[k].astype(F32)
    drift_out[...] = summed * (1.0 / NI)

    await_recv(gw.at[pl.ds(1, 3), 0, 0, half], g_send.at[0])
    await_recv(gw.at[:, 0, pl.ds(1, 3), half], g_send.at[1])
    await_recv(gw.at[:, first, :, half], g_send.at[2])
    await_recv(gw.at[:, 2, :, half], g_send.at[3])
    await_recv(gw.at[:, :, :, half], g_send.at[4])
    for k in range(1, NI):
        await_recv(diffs.at[0], d_send.at[k])
    await_recv(s_a, rs_send.at[0])
    await_recv(s_bp, rs_send.at[1])
    await_recv(s_bm, rs_send.at[2])
    await_recv(s_z, rs_send.at[3])
    await_recv(s_h.at[pl.ds(1, 3)], rs_send.at[4])
    await_recv(total.at[other], tail_send)

    await_recv(r_x, tail_recv)
    usum_out[...] = total[half, :] + r_x[...]


def adam_step(param, grad, first, second):
    first = BETA_ONE * first + (1.0 - BETA_ONE) * grad
    second = BETA_TWO * second + (1.0 - BETA_TWO) * grad * grad
    param = param - INNER_LR * (first / (jnp.sqrt(second) + ADAM_EPS) + DECAY * param)
    return (param, first, second)


def update(
    keys,
    unit_sum,
    drift,
    weight,
    weight_m,
    weight_v,
    gain,
    gain_m,
    gain_v,
    outer,
    momentum,
    fragment,
    active,
    keys_out,
    weight_out,
    weight_m_out,
    weight_v_out,
    gain_out,
    gain_m_out,
    gain_v_out,
    outer_out,
    momentum_out,
):
    key_scale = WIDTH ** (-0.5)
    eye = lax.broadcasted_iota(jnp.int32, (ROWS, ROWS), 0) == lax.broadcasted_iota(
        jnp.int32, (ROWS, ROWS), 1
    )

    def to_column(row):
        return jnp.sum(jnp.where(eye, row, jnp.zeros_like(row)), axis=1, keepdims=True)

    keys_out[...] = keys[...].astype(BF16)
    w, sums = weight[0], unit_sum[...]
    gain_bf = gain[...].astype(BF16).astype(F32)
    weight_grad = key_scale * to_column(gain_bf) * sums
    column = jnp.sum(w.astype(BF16).astype(F32) * sums, axis=1, keepdims=True)
    gain_grad = key_scale * jnp.sum(jnp.where(eye, column, 0.0), axis=0, keepdims=True)
    inner, first, second = adam_step(w, weight_grad, weight_m[0], weight_v[0])
    weight_m_out[0], weight_v_out[0] = first, second
    new, first, second = adam_step(gain[...], gain_grad, gain_m[...], gain_v[...])
    gain_out[...], gain_m_out[...], gain_v_out[...] = new, first, second
    pushed = OUTER_MU * momentum[...] + drift[...]
    candidate = outer[...] - OUTER_LR * (OUTER_MU * pushed + drift[...])
    current = lax.rem(active[0], NFRAG)
    chosen = jnp.where(fragment[...] == current, 1.0, 0.0)
    in_fragment = jnp.broadcast_to(to_column(chosen), (ROWS, HEAD)) > 0.5
    momentum_out[...] = jnp.where(in_fragment, pushed, momentum[...])
    outer_out[...] = jnp.where(in_fragment, candidate, outer[...])
    weight_out[0] = jnp.where(
        in_fragment, MIX_KEEP * inner + (1.0 - MIX_KEEP) * candidate, inner
    )


def shards(
    tokens,
    key_grad,
    weight,
    weight_m,
    weight_v,
    gain,
    gain_m,
    gain_v,
    outer,
    momentum,
    fragment_of_row,
    active_fragment,
):
    vmem = pl.BlockSpec(memory_space=pltpu.VMEM)
    block = (HEAD, BLOCK)
    dma = pltpu.SemaphoreType.DMA
    keys, unit_sum, outer_drift = pl.pallas_call(
        exchange,
        out_shape=(
            pltpu.VMEM((TOK, HEAD), F32),
            pltpu.VMEM((ROWS, HEAD), F32),
            pltpu.VMEM((ROWS, HEAD), F32),
        ),
        in_specs=[pl.BlockSpec(memory_space=pl.ANY)] * 5,
        out_specs=(vmem, vmem, vmem),
        scratch_shapes=[
            pltpu.VMEM((4, TOK, GROUP), BF16),
            pltpu.VMEM((4, NY, 4, BLOCK, HEAD), BF16),
            pltpu.VMEM((4, HEAD, GROUP), F32),
            *[pltpu.VMEM((4, 4) + block, BF16)] * 6,
            *[pltpu.VMEM((4, 3) + block, BF16)] * 2,
            *[pltpu.VMEM((4,) + block, BF16)] * 2,
            pltpu.VMEM((4,) + block, F32),
            pltpu.VMEM(block, F32),
            pltpu.VMEM((ROWS, HEAD), F32),
            pltpu.VMEM((NI, ROWS, HEAD), BF16),
            pltpu.VMEM((TOK, HEAD), F32),
            pltpu.VMEM((HEAD, TOK), BF16),
            pltpu.VMEM((TOK, HEAD), F32),
            pltpu.VMEM((TOK, HEAD), BF16),
            pltpu.VMEM((1, ROWS, HEAD), F32),
            pltpu.VMEM((1, ROWS), F32),
            pltpu.VMEM((ROWS, HEAD), F32),
            dma((4,)),
            dma((4,)),
            dma((4,)),
            dma((4, 4)),
            dma((4, 4)),
            dma((4, 4)),
            dma((5,)),
            dma((4, 2)),
            dma((4, 2)),
            dma((4, 3)),
            dma((4,)),
            dma((5,)),
            dma,
            dma,
            dma((NI,)),
            dma((NI,)),
        ],
        compiler_params=pltpu.CompilerParams(
            collective_id=0, has_side_effects=True, vmem_limit_bytes=60 * 2**20
        ),
        cost_estimate=pl.CostEstimate(
            flops=4 * TOK * WIDTH * HEAD, bytes_accessed=2 * TOK * WIDTH, transcendentals=0
        ),
    )(tokens, key_grad, weight, gain, outer)
    state = (ROWS, HEAD)
    results = pl.pallas_call(
        update,
        out_shape=(
            jax.ShapeDtypeStruct((TOK, HEAD), BF16),
            jax.ShapeDtypeStruct((1,) + state, F32),
            jax.ShapeDtypeStruct((1,) + state, F32),
            jax.ShapeDtypeStruct((1,) + state, F32),
            jax.ShapeDtypeStruct((1, ROWS), F32),
            jax.ShapeDtypeStruct((1, ROWS), F32),
            jax.ShapeDtypeStruct((1, ROWS), F32),
            jax.ShapeDtypeStruct(state, F32),
            jax.ShapeDtypeStruct(state, F32),
        ),
        in_specs=[vmem] * 12 + [pl.BlockSpec(memory_space=pltpu.SMEM)],
        out_specs=(vmem,) * 9,
        compiler_params=pltpu.CompilerParams(vmem_limit_bytes=4 * 2**20),
    )(
        keys,
        unit_sum,
        outer_drift,
        weight,
        weight_m,
        weight_v,
        gain,
        gain_m,
        gain_v,
        outer,
        momentum,
        fragment_of_row[None],
        active_fragment,
    )
    return results


def solution(mesh):
    return jax.shard_map(
        shards,
        mesh=mesh,
        in_specs=(
            P(("island", "fsdp"), None),
            P(("island", "fsdp"), None),
            P("island", "fsdp", None),
            P("island", "fsdp", None),
            P("island", "fsdp", None),
            P("island", "fsdp"),
            P("island", "fsdp"),
            P("island", "fsdp"),
            P("fsdp", None),
            P("fsdp", None),
            P("fsdp"),
            P(),
        ),
        out_specs=(
            P(("island", "fsdp"), None),
            P("island", "fsdp", None),
            P("island", "fsdp", None),
            P("island", "fsdp", None),
            P("island", "fsdp"),
            P("island", "fsdp"),
            P("island", "fsdp"),
            P("fsdp", None),
            P("fsdp", None),
        ),
        check_vma=False,
    )
```

```python
import jax
import jax.numpy as jnp
from jax import lax
from jax.experimental import pallas as pl
from jax.experimental.pallas import tpu as pltpu
from jax.sharding import PartitionSpec as P

NFRAG = 4
NORM_EPS = 1e-05
BETA_ONE = 0.9
BETA_TWO = 0.999
ADAM_EPS = 1e-08
INNER_LR = 0.01
DECAY = 0.1
OUTER_LR = 0.7
OUTER_MU = 0.9
MIX_KEEP = 0.5

MESH = pl.DeviceIdType.MESH
NY, NZ, NX, NI = 4, 16, 2, 4
TOK, WIDTH, HEAD = 256, 8192, 128
ROWS = 64
BLOCK = NX * ROWS
ZSTEP = (0, 1, -2, -1)
EARLY = 16
DIRECT = 2
ORDER = (2, 1, 3, 0)
GROUP = NY * 4 * BLOCK
F32, BF16 = jnp.float32, jnp.bfloat16


def exchange(
    x_hbm,
    kg_hbm,
    weight_hbm,
    gain_hbm,
    outer_hbm,
    keys_out,
    usum_out,
    drift_out,
    xv,
    gw,
    part,
    s_a,
    r_a,
    s_bp,
    s_bm,
    r_bp,
    r_bm,
    s_z,
    r_z,
    s_h,
    own,
    s_o,
    r_t,
    diffs,
    acc,
    kgt,
    inv,
    kg,
    weight,
    gain,
    outer,
    sem_in,
    sem_x,
    gh_recv,
    gz_recv,
    gy_recv,
    gx_recv,
    ty_recv,
    th_recv,
    tz_recv,
    g_send,
    a_recv,
    b_recv,
    z_recv,
    rs_send,
    tail_send,
    t_recv,
    d_send,
    d_recv,
):
    isl, f = lax.axis_index("island"), lax.axis_index("fsdp")
    y, z, xl = f // (NZ * NX), (f // NX) % NZ, f % NX

    def device(dy=0, dz=0, flip=False):
        yy, zz = (y + NY + dy) % NY, (z + NZ + dz) % NZ
        xx = 1 - xl if flip else xl
        return (isl, (yy * NZ + zz) * NX + xx)

    loads = [
        pltpu.make_async_copy(src, dst, sem_in.at[k])
        for k, (src, dst) in enumerate(
            [(weight_hbm, weight), (gain_hbm, gain), (outer_hbm, outer), (kg_hbm, kg)]
        )
    ]
    for copy in loads:
        copy.start()
    up_y, down_y = device(dy=1), device(dy=-1)
    near = {d: device(dz=d) for d in (1, -1, 2, -2)}
    far = {k: device(dz=d) for k, d in ((1, 4), (2, 8), (3, -4))}
    near_flip = {d: device(dz=d, flip=True) for d in (1, -1, 2, -2)}
    far_flip = {k: device(dz=d, flip=True) for k, d in ((1, 4), (2, 8), (3, -4))}
    opposite_y = device(dy=2)
    partner = device(flip=True)
    islands = [((isl + k) % NI, f) for k in range(1, NI)]

    barrier = pltpu.get_barrier_semaphore()
    peers = [up_y, down_y, opposite_y, partner] + islands
    for group in (near, far, near_flip, far_flip):
        peers += list(group.values())
    for peer in peers:
        pl.semaphore_signal(barrier, inc=1, device_id=peer, device_id_type=MESH)

    def load(k):
        def one(q, carry):
            for j in range(4):
                block = ((y + q) % NY) * NZ + (z + NZ + 4 * k + ZSTEP[j]) % NZ
                pltpu.make_async_copy(
                    x_hbm.at[:, pl.ds(pl.multiple_of(block * BLOCK, BLOCK), BLOCK)],
                    xv.at[k, :, pl.ds(pl.multiple_of((q * 4 + j) * BLOCK, BLOCK), BLOCK)],
                    sem_x.at[k],
                ).start()
            return carry

        lax.fori_loop(0, NY, one, 0)

    for k in ORDER:
        load(k)

    def remote(src, dst, send, recv, to):
        return pltpu.make_async_remote_copy(
            src_ref=src,
            dst_ref=dst,
            send_sem=send,
            recv_sem=recv,
            device_id=to,
            device_id_type=MESH,
        )

    def await_recv(ref, sem):
        pltpu.make_async_copy(ref, ref, sem).wait()

    half = pl.ds(pl.multiple_of(xl * ROWS, ROWS), ROWS)
    other = pl.ds(pl.multiple_of((1 - xl) * ROWS, ROWS), ROWS)
    main = pl.ds(pl.multiple_of(xl * ROWS, ROWS), ROWS - EARLY)
    early = pl.ds(pl.multiple_of(xl * ROWS + ROWS - EARLY, EARLY), EARLY)
    first, last = pl.ds(0, 2), pl.ds(2, 2)

    for copy in loads[:3]:
        copy.wait()
    eye = lax.broadcasted_iota(jnp.int32, (ROWS, ROWS), 0) == lax.broadcasted_iota(
        jnp.int32, (ROWS, ROWS), 1
    )
    gain_bf = gain[...].astype(BF16).astype(F32)
    column = jnp.sum(jnp.where(eye, gain_bf, 0.0), axis=1, keepdims=True)
    w = weight[0]
    gw[0, 0, 0, half, :] = (column * w.astype(BF16).astype(F32)).astype(BF16)
    diffs[isl] = (outer[...] - w).astype(BF16)

    def send_far(k):
        remote(
            gw.at[0, 0, 0, main], gw.at[4 - k, 0, 0, main], g_send.at[0], gh_recv.at[4 - k], far[k]
        ).start()

    def wait_far(k):
        await_recv(gw.at[k, 0, 0, main], gh_recv.at[k])

    def send_near(k):
        for j, d in ((2, 2), (3, 1), (1, -1)):
            remote(
                gw.at[k, 0, 0, main], gw.at[k, 0, j, main], g_send.at[1], gz_recv.at[k, j], near[d]
            ).start()

    def early_y():
        mine = gw.at[0, 0, 0, early]
        for q, to in ((3, up_y), (1, down_y), (2, opposite_y)):
            remote(mine, gw.at[0, q, 0, early], g_send.at[5], ty_recv.at[q], to).start()

    def early_near(k):
        for j, d in ((2, 2), (3, 1), (1, -1)):
            remote(
                gw.at[k, :, 0, early], gw.at[k, :, j, early], g_send.at[7], tz_recv.at[k, j], near[d]
            ).start()

    def early_z():
        for q in (1, 2, 3):
            await_recv(gw.at[0, q, 0, early], ty_recv.at[q])
        for k in (2, 1, 3):
            remote(
                gw.at[0, :, 0, early],
                gw.at[4 - k, :, 0, early],
                g_send.at[6],
                th_recv.at[4 - k],
                far[k],
            ).start()
        early_near(0)

    def early_far(k):
        await_recv(gw.at[k, :, 0, early], th_recv.at[k])
        early_near(k)

    def early_x(k):
        for j in (1, 2, 3):
            await_recv(gw.at[k, :, j, early], tz_recv.at[k, j])
        send_x(k, 0)

    def send_x(k, q):
        block = gw.at[k, q, :, half]
        remote(block, block, g_send.at[4], gx_recv.at[k, q], partner).start()

    def send_y(k):
        for j in (1, 3, 2):
            await_recv(gw.at[k, 0, j, main], gz_recv.at[k, j])
        block = gw.at[k, 0, :, main]
        remote(block, gw.at[k, 3, :, main], g_send.at[2], gy_recv.at[k, 3], up_y).start()
        remote(block, gw.at[k, 1, :, main], g_send.at[2], gy_recv.at[k, 1], down_y).start()
        if k == DIRECT:
            remote(
                block, gw.at[k, 2, :, main], g_send.at[3], gy_recv.at[k, 2], opposite_y
            ).start()

    def forward_y(k):
        for q, part_j, slot, to in ((3, first, 0, up_y), (1, last, 2, down_y)):
            await_recv(gw.at[k, q, :, main], gy_recv.at[k, q])
            if k != DIRECT:
                remote(
                    gw.at[k, q, part_j, main],
                    gw.at[k, 2, part_j, main],
                    g_send.at[3],
                    gy_recv.at[k, slot],
                    to,
                ).start()
            send_x(k, q)

    def opposite(k):
        if k == DIRECT:
            await_recv(gw.at[k, 2, :, main], gy_recv.at[k, 2])
        else:
            await_recv(gw.at[k, 2, first, main], gy_recv.at[k, 0])
            await_recv(gw.at[k, 2, last, main], gy_recv.at[k, 2])
        send_x(k, 2)

    def keys_part(k, q):
        await_recv(gw.at[k, q, :, other], gx_recv.at[k, q])
        columns = pl.ds(q * 4 * BLOCK, 4 * BLOCK)
        acc[...] += jnp.dot(
            xv[k, :, columns], gw[k, q].reshape(4 * BLOCK, HEAD), preferred_element_type=F32
        )

    def block_of(k, q, j):
        start = (q * 4 + j) * BLOCK
        return part[k, start : start + BLOCK]

    def step_one(k):
        part[k] = lax.dot_general(
            xv[k], kgt[...], (((0,), (0,)), ((), ())), preferred_element_type=F32
        )
        for j in range(4):
            s_a[k, j] = block_of(k, 2, j).astype(BF16)
        remote(s_a.at[k, first], r_a.at[k, first], rs_send.at[0], a_recv.at[k, 0], up_y).start()
        remote(s_a.at[k, last], r_a.at[k, last], rs_send.at[0], a_recv.at[k, 1], down_y).start()

    def step_two(k):
        await_recv(r_a.at[k, first], a_recv.at[k, 0])
        for j in range(4):
            mine = block_of(k, 1, j)
            s_bp[k, j] = (mine + r_a[k, j].astype(F32) if j < 2 else mine).astype(BF16)
        remote(s_bp.at[k], r_bp.at[k], rs_send.at[1], b_recv.at[k, 0], up_y).start()
        await_recv(r_a.at[k, last], a_recv.at[k, 1])
        for j in range(4):
            mine = block_of(k, 3, j)
            s_bm[k, j] = (mine if j < 2 else mine + r_a[k, j].astype(F32)).astype(BF16)
        remote(s_bm.at[k], r_bm.at[k], rs_send.at[2], b_recv.at[k, 1], down_y).start()

    def split(block, place, send, key, same, flipped):
        for rows, slot, to in ((half, place, same[key]), (other, place + 1, flipped[key])):
            remote(block.at[rows], r_t.at[slot], send, t_recv.at[slot], to).start()

    def step_three(k):
        await_recv(r_bp.at[k], b_recv.at[k, 0])
        await_recv(r_bm.at[k], b_recv.at[k, 1])
        for j in (2, 1, 3, 0):
            summed = block_of(k, 0, j) + r_bp[k, j].astype(F32) + r_bm[k, j].astype(F32)
            if j == 0:
                own[k] = summed
                if k == 0:
                    s_o[...] = summed.astype(BF16)
                    remote(s_o.at[other], r_t.at[12], tail_send, t_recv.at[12], partner).start()
                continue
            s_z[k, j - 1] = summed.astype(BF16)
            if k == 0:
                split(s_z.at[0, j - 1], 2 * j - 2, rs_send.at[3], ZSTEP[j], near, near_flip)
            else:
                remote(
                    s_z.at[k, j - 1],
                    r_z.at[k, j - 1],
                    rs_send.at[3],
                    z_recv.at[k, j - 1],
                    near[ZSTEP[j]],
                ).start()

    def step_four(k):
        summed = own[k]
        for j in range(3):
            await_recv(r_z.at[k, j], z_recv.at[k, j])
            summed = summed + r_z[k, j].astype(F32)
        s_h[k] = summed.astype(BF16)
        split(s_h.at[k], 4 + 2 * k, rs_send.at[4], k, far, far_flip)

    inv[...] = jnp.zeros_like(inv)
    acc[...] = jnp.zeros_like(acc)
    for k in ORDER:
        await_recv(xv.at[k], sem_x.at[k])

        def squares(q, carry):
            for j in range(4):
                lanes = pl.ds(pl.multiple_of((q * 4 + j) * BLOCK, BLOCK), BLOCK)
                v = xv[k, :, lanes].astype(F32)
                inv[...] += v * v
            return carry

        lax.fori_loop(0, NY, squares, 0)
    scale = lax.rsqrt(jnp.sum(inv[...], axis=1, keepdims=True) * (1.0 / WIDTH) + NORM_EPS)
    inv[...] = jnp.broadcast_to(scale, inv.shape)
    loads[3].wait()
    kgt[...] = (kg[...].astype(F32) * inv[...]).astype(BF16)

    pl.semaphore_wait(barrier, len(peers))
    early_y()
    for k in (2, 1, 3):
        send_far(k)
    send_near(0)
    for k in range(1, NI):
        remote(
            diffs.at[isl], diffs.at[isl], d_send.at[k], d_recv.at[NI - k], islands[k - 1]
        ).start()

    for k in ORDER:
        step_one(k)
    send_y(0)
    early_z()
    wait_far(1)
    send_near(1)
    wait_far(3)
    send_near(3)
    step_two(2)
    wait_far(2)
    send_near(2)
    step_two(1)
    early_x(0)
    send_y(1)
    send_y(3)
    early_far(1)
    early_far(3)
    forward_y(0)
    send_y(2)
    early_far(2)
    step_two(3)
    early_x(1)
    early_x(3)
    early_x(2)
    forward_y(1)
    forward_y(3)
    step_two(0)
    step_three(2)
    opposite(0)
    forward_y(2)
    step_three(1)
    step_four(2)
    opposite(1)
    opposite(3)
    opposite(2)
    step_three(3)
    step_four(1)
    keys_part(0, 0)
    keys_part(0, 1)
    keys_part(0, 3)
    keys_part(1, 0)
    keys_part(3, 0)
    keys_part(2, 0)
    step_three(0)
    step_four(3)
    keys_part(1, 1)
    keys_part(1, 3)
    keys_part(3, 1)
    keys_part(3, 3)
    keys_part(0, 2)
    keys_part(2, 1)
    keys_part(2, 3)
    keys_part(1, 2)
    keys_part(3, 2)
    keys_part(2, 2)

    keys_out[...] = acc[...] * (inv[...] * WIDTH ** (-0.5))
    for k in range(1, NI):
        await_recv(diffs.at[(isl + k) % NI], d_recv.at[k])
    summed = diffs[0].astype(F32)
    for k in range(1, NI):
        summed = summed + diffs[k].astype(F32)
    drift_out[...] = summed * (1.0 / NI)

    await_recv(gw.at[pl.ds(1, 3), 0, 0, main], g_send.at[0])
    await_recv(gw.at[:, 0, pl.ds(1, 3), main], g_send.at[1])
    await_recv(gw.at[:, first, :, main], g_send.at[2])
    await_recv(gw.at[:, 2, :, main], g_send.at[3])
    await_recv(gw.at[:, :, :, half], g_send.at[4])
    await_recv(gw.at[0, pl.ds(1, 3), 0, early], g_send.at[5])
    await_recv(gw.at[pl.ds(1, 3), :, 0, early], g_send.at[6])
    await_recv(gw.at[:, :, pl.ds(1, 3), early], g_send.at[7])
    for k in range(1, NI):
        await_recv(diffs.at[0], d_send.at[k])
    await_recv(s_a, rs_send.at[0])
    await_recv(s_bp, rs_send.at[1])
    await_recv(s_bm, rs_send.at[2])
    await_recv(s_z, rs_send.at[3])
    await_recv(s_h.at[pl.ds(1, 3)], rs_send.at[4])
    await_recv(s_o.at[other], tail_send)

    summed = own[0, half, :]
    for slot in range(13):
        await_recv(r_t.at[slot], t_recv.at[slot])
        summed = summed + r_t[slot].astype(F32)
    usum_out[...] = summed


def adam_step(param, grad, first, second):
    first = BETA_ONE * first + (1.0 - BETA_ONE) * grad
    second = BETA_TWO * second + (1.0 - BETA_TWO) * grad * grad
    param = param - INNER_LR * (first / (jnp.sqrt(second) + ADAM_EPS) + DECAY * param)
    return (param, first, second)


def update(
    keys,
    unit_sum,
    drift,
    weight,
    weight_m,
    weight_v,
    gain,
    gain_m,
    gain_v,
    outer,
    momentum,
    fragment,
    active,
    keys_out,
    weight_out,
    weight_m_out,
    weight_v_out,
    gain_out,
    gain_m_out,
    gain_v_out,
    outer_out,
    momentum_out,
):
    key_scale = WIDTH ** (-0.5)
    eye = lax.broadcasted_iota(jnp.int32, (ROWS, ROWS), 0) == lax.broadcasted_iota(
        jnp.int32, (ROWS, ROWS), 1
    )

    def to_column(row):
        return jnp.sum(jnp.where(eye, row, jnp.zeros_like(row)), axis=1, keepdims=True)

    keys_out[...] = keys[...].astype(BF16)
    w, sums = weight[0], unit_sum[...]
    gain_bf = gain[...].astype(BF16).astype(F32)
    weight_grad = key_scale * to_column(gain_bf) * sums
    column = jnp.sum(w.astype(BF16).astype(F32) * sums, axis=1, keepdims=True)
    gain_grad = key_scale * jnp.sum(jnp.where(eye, column, 0.0), axis=0, keepdims=True)
    inner, first, second = adam_step(w, weight_grad, weight_m[0], weight_v[0])
    weight_m_out[0], weight_v_out[0] = first, second
    new, first, second = adam_step(gain[...], gain_grad, gain_m[...], gain_v[...])
    gain_out[...], gain_m_out[...], gain_v_out[...] = new, first, second
    pushed = OUTER_MU * momentum[...] + drift[...]
    candidate = outer[...] - OUTER_LR * (OUTER_MU * pushed + drift[...])
    current = lax.rem(active[...], NFRAG)
    chosen = jnp.where(fragment[...] == current, 1.0, 0.0)
    in_fragment = jnp.broadcast_to(to_column(chosen), (ROWS, HEAD)) > 0.5
    momentum_out[...] = jnp.where(in_fragment, pushed, momentum[...])
    outer_out[...] = jnp.where(in_fragment, candidate, outer[...])
    weight_out[0] = jnp.where(
        in_fragment, MIX_KEEP * inner + (1.0 - MIX_KEEP) * candidate, inner
    )


def shards(
    tokens,
    key_grad,
    weight,
    weight_m,
    weight_v,
    gain,
    gain_m,
    gain_v,
    outer,
    momentum,
    fragment_of_row,
    active_fragment,
):
    vmem = pl.BlockSpec(memory_space=pltpu.VMEM)
    block = (HEAD, BLOCK)
    dma = pltpu.SemaphoreType.DMA
    keys, unit_sum, outer_drift = pl.pallas_call(
        exchange,
        out_shape=(
            pltpu.VMEM((TOK, HEAD), F32),
            pltpu.VMEM((ROWS, HEAD), F32),
            pltpu.VMEM((ROWS, HEAD), F32),
        ),
        in_specs=[pl.BlockSpec(memory_space=pl.ANY)] * 5,
        out_specs=(vmem, vmem, vmem),
        scratch_shapes=[
            pltpu.VMEM((4, TOK, GROUP), BF16),
            pltpu.VMEM((4, NY, 4, BLOCK, HEAD), BF16),
            pltpu.VMEM((4, GROUP, HEAD), F32),
            *[pltpu.VMEM((4, 4) + block, BF16)] * 6,
            *[pltpu.VMEM((4, 3) + block, BF16)] * 2,
            pltpu.VMEM((4,) + block, BF16),
            pltpu.VMEM((4,) + block, F32),
            pltpu.VMEM(block, BF16),
            pltpu.VMEM((13, ROWS, HEAD), BF16),
            pltpu.VMEM((NI, ROWS, HEAD), BF16),
            pltpu.VMEM((TOK, HEAD), F32),
            pltpu.VMEM((TOK, HEAD), BF16),
            pltpu.VMEM((TOK, HEAD), F32),
            pltpu.VMEM((TOK, HEAD), BF16),
            pltpu.VMEM((1, ROWS, HEAD), F32),
            pltpu.VMEM((1, ROWS), F32),
            pltpu.VMEM((ROWS, HEAD), F32),
            dma((4,)),
            dma((4,)),
            dma((4,)),
            dma((4, 4)),
            dma((4, 4)),
            dma((4, 4)),
            dma((NY,)),
            dma((4,)),
            dma((4, 4)),
            dma((8,)),
            dma((4, 2)),
            dma((4, 2)),
            dma((4, 3)),
            dma((5,)),
            dma,
            dma((13,)),
            dma((NI,)),
            dma((NI,)),
        ],
        compiler_params=pltpu.CompilerParams(
            collective_id=0, has_side_effects=True, vmem_limit_bytes=60 * 2**20
        ),
        cost_estimate=pl.CostEstimate(
            flops=4 * TOK * WIDTH * HEAD, bytes_accessed=2 * TOK * WIDTH, transcendentals=0
        ),
    )(tokens, key_grad, weight, gain, outer)
    state = (ROWS, HEAD)
    results = pl.pallas_call(
        update,
        out_shape=(
            jax.ShapeDtypeStruct((TOK, HEAD), BF16),
            jax.ShapeDtypeStruct((1,) + state, F32),
            jax.ShapeDtypeStruct((1,) + state, F32),
            jax.ShapeDtypeStruct((1,) + state, F32),
            jax.ShapeDtypeStruct((1, ROWS), F32),
            jax.ShapeDtypeStruct((1, ROWS), F32),
            jax.ShapeDtypeStruct((1, ROWS), F32),
            jax.ShapeDtypeStruct(state, F32),
            jax.ShapeDtypeStruct(state, F32),
        ),
        in_specs=[vmem] * 13,
        out_specs=(vmem,) * 9,
        compiler_params=pltpu.CompilerParams(vmem_limit_bytes=4 * 2**20),
    )(
        keys,
        unit_sum,
        outer_drift,
        weight,
        weight_m,
        weight_v,
        gain,
        gain_m,
        gain_v,
        outer,
        momentum,
        fragment_of_row[None],
        active_fragment[None],
    )
    return results


def solution(mesh):
    return jax.shard_map(
        shards,
        mesh=mesh,
        in_specs=(
            P(("island", "fsdp"), None),
            P(("island", "fsdp"), None),
            P("island", "fsdp", None),
            P("island", "fsdp", None),
            P("island", "fsdp", None),
            P("island", "fsdp"),
            P("island", "fsdp"),
            P("island", "fsdp"),
            P("fsdp", None),
            P("fsdp", None),
            P("fsdp"),
            P(),
        ),
        out_specs=(
            P(("island", "fsdp"), None),
            P("island", "fsdp", None),
            P("island", "fsdp", None),
            P("island", "fsdp", None),
            P("island", "fsdp"),
            P("island", "fsdp"),
            P("island", "fsdp"),
            P("fsdp", None),
            P("fsdp", None),
        ),
        check_vma=False,
    )
```

```python
import jax
import jax.numpy as jnp
from jax import lax
from jax.experimental import pallas as pl
from jax.experimental.pallas import tpu as pltpu
from jax.sharding import PartitionSpec as P

NFRAG = 4
NORM_EPS = 1e-05
BETA_ONE = 0.9
BETA_TWO = 0.999
ADAM_EPS = 1e-08
INNER_LR = 0.01
DECAY = 0.1
OUTER_LR = 0.7
OUTER_MU = 0.9
MIX_KEEP = 0.5

MESH = pl.DeviceIdType.MESH
NY, NZ, NX, NI = 4, 16, 2, 4
TOK, WIDTH, HEAD = 256, 8192, 128
ROWS = 64
BLOCK = NX * ROWS
ZSTEP = (0, 1, -2, -1)
EARLY = 16
ORDER = (2, 1, 3, 0)
GROUP = NY * 4 * BLOCK
F32, BF16 = jnp.float32, jnp.bfloat16


def exchange(
    x_hbm,
    kg_hbm,
    weight_hbm,
    gain_hbm,
    outer_hbm,
    keys_out,
    usum_out,
    drift_out,
    xv,
    gw,
    part,
    s_a,
    r_a,
    s_bp,
    s_bm,
    r_bp,
    r_bm,
    s_z,
    r_z,
    s_h,
    own,
    s_o,
    r_t,
    diffs,
    acc,
    kgt,
    inv,
    kg,
    weight,
    gain,
    outer,
    sem_in,
    sem_x,
    gh_recv,
    gz_recv,
    gy_recv,
    gx_recv,
    ty_recv,
    th_recv,
    tz_recv,
    g_send,
    a_recv,
    b_recv,
    z_recv,
    rs_send,
    tail_send,
    t_recv,
    d_send,
    d_recv,
):
    isl, f = lax.axis_index("island"), lax.axis_index("fsdp")
    y, z, xl = f // (NZ * NX), (f // NX) % NZ, f % NX

    def device(dy=0, dz=0, flip=False):
        yy, zz = (y + NY + dy) % NY, (z + NZ + dz) % NZ
        xx = 1 - xl if flip else xl
        return (isl, (yy * NZ + zz) * NX + xx)

    loads = [
        pltpu.make_async_copy(src, dst, sem_in.at[k])
        for k, (src, dst) in enumerate(
            [(weight_hbm, weight), (gain_hbm, gain), (outer_hbm, outer), (kg_hbm, kg)]
        )
    ]
    for copy in loads:
        copy.start()
    up_y, down_y = device(dy=1), device(dy=-1)
    near = {d: device(dz=d) for d in (1, -1, 2, -2)}
    far = {k: device(dz=d) for k, d in ((1, 4), (2, 8), (3, -4))}
    near_flip = {d: device(dz=d, flip=True) for d in (1, -1, 2, -2)}
    far_flip = {k: device(dz=d, flip=True) for k, d in ((1, 4), (2, 8), (3, -4))}
    opposite_y = device(dy=2)
    partner = device(flip=True)
    islands = [((isl + k) % NI, f) for k in range(1, NI)]

    barrier = pltpu.get_barrier_semaphore()
    peers = [up_y, down_y, opposite_y, partner] + islands
    for group in (near, far, near_flip, far_flip):
        peers += list(group.values())
    for peer in peers:
        pl.semaphore_signal(barrier, inc=1, device_id=peer, device_id_type=MESH)

    def load(k):
        def one(q, carry):
            for j in range(4):
                block = ((y + q) % NY) * NZ + (z + NZ + 4 * k + ZSTEP[j]) % NZ
                pltpu.make_async_copy(
                    x_hbm.at[:, pl.ds(pl.multiple_of(block * BLOCK, BLOCK), BLOCK)],
                    xv.at[k, :, pl.ds(pl.multiple_of((q * 4 + j) * BLOCK, BLOCK), BLOCK)],
                    sem_x.at[k],
                ).start()
            return carry

        lax.fori_loop(0, NY, one, 0)

    for k in ORDER:
        load(k)

    def remote(src, dst, send, recv, to):
        return pltpu.make_async_remote_copy(
            src_ref=src,
            dst_ref=dst,
            send_sem=send,
            recv_sem=recv,
            device_id=to,
            device_id_type=MESH,
        )

    def await_recv(ref, sem):
        pltpu.make_async_copy(ref, ref, sem).wait()

    half = pl.ds(pl.multiple_of(xl * ROWS, ROWS), ROWS)
    other = pl.ds(pl.multiple_of((1 - xl) * ROWS, ROWS), ROWS)
    main = pl.ds(pl.multiple_of(xl * ROWS, ROWS), ROWS - EARLY)
    early = pl.ds(pl.multiple_of(xl * ROWS + ROWS - EARLY, EARLY), EARLY)
    first, last = pl.ds(0, 2), pl.ds(2, 2)

    for copy in loads[:3]:
        copy.wait()
    eye = lax.broadcasted_iota(jnp.int32, (ROWS, ROWS), 0) == lax.broadcasted_iota(
        jnp.int32, (ROWS, ROWS), 1
    )
    gain_bf = gain[...].astype(BF16).astype(F32)
    column = jnp.sum(jnp.where(eye, gain_bf, 0.0), axis=1, keepdims=True)
    w = weight[0]
    gw[0, 0, 0, half, :] = (column * w.astype(BF16).astype(F32)).astype(BF16)
    diffs[isl] = (outer[...] - w).astype(BF16)

    def send_far(k):
        remote(
            gw.at[0, 0, 0, main], gw.at[4 - k, 0, 0, main], g_send.at[0], gh_recv.at[4 - k], far[k]
        ).start()

    def wait_far(k):
        await_recv(gw.at[k, 0, 0, main], gh_recv.at[k])

    def send_near(k):
        for j, d in ((2, 2), (3, 1), (1, -1)):
            remote(
                gw.at[k, 0, 0, main], gw.at[k, 0, j, main], g_send.at[1], gz_recv.at[k, j], near[d]
            ).start()

    def early_y():
        mine = gw.at[0, 0, 0, early]
        for q, to in ((3, up_y), (1, down_y), (2, opposite_y)):
            remote(mine, gw.at[0, q, 0, early], g_send.at[5], ty_recv.at[q], to).start()

    def early_near(k):
        for j, d in ((2, 2), (3, 1), (1, -1)):
            remote(
                gw.at[k, :, 0, early], gw.at[k, :, j, early], g_send.at[7], tz_recv.at[k, j], near[d]
            ).start()

    def early_z():
        for q in (1, 2, 3):
            await_recv(gw.at[0, q, 0, early], ty_recv.at[q])
        for k in (2, 1, 3):
            remote(
                gw.at[0, :, 0, early],
                gw.at[4 - k, :, 0, early],
                g_send.at[6],
                th_recv.at[4 - k],
                far[k],
            ).start()
        early_near(0)

    def early_far(k):
        await_recv(gw.at[k, :, 0, early], th_recv.at[k])
        early_near(k)

    def early_x(k):
        for j in (1, 2, 3):
            await_recv(gw.at[k, :, j, early], tz_recv.at[k, j])
        send_x(k, 0)

    def send_x(k, q):
        block = gw.at[k, q, :, half]
        remote(block, block, g_send.at[4], gx_recv.at[k, q], partner).start()

    def send_y(k):
        for j in (1, 3, 2):
            await_recv(gw.at[k, 0, j, main], gz_recv.at[k, j])
        block = gw.at[k, 0, :, main]
        remote(block, gw.at[k, 3, :, main], g_send.at[2], gy_recv.at[k, 3], up_y).start()
        remote(block, gw.at[k, 1, :, main], g_send.at[2], gy_recv.at[k, 1], down_y).start()

    def forward_y(k):
        for q, part_j, slot, to in ((3, first, 0, up_y), (1, last, 2, down_y)):
            await_recv(gw.at[k, q, :, main], gy_recv.at[k, q])
            remote(
                gw.at[k, q, part_j, main],
                gw.at[k, 2, part_j, main],
                g_send.at[3],
                gy_recv.at[k, slot],
                to,
            ).start()
            send_x(k, q)

    def opposite(k):
        await_recv(gw.at[k, 2, first, main], gy_recv.at[k, 0])
        await_recv(gw.at[k, 2, last, main], gy_recv.at[k, 2])
        send_x(k, 2)

    def keys_part(k, q):
        await_recv(gw.at[k, q, :, other], gx_recv.at[k, q])
        columns = pl.ds(q * 4 * BLOCK, 4 * BLOCK)
        acc[...] += jnp.dot(
            xv[k, :, columns], gw[k, q].reshape(4 * BLOCK, HEAD), preferred_element_type=F32
        )

    def block_of(k, q, j):
        start = (q * 4 + j) * BLOCK
        return part[k, start : start + BLOCK]

    def step_one(k):
        part[k] = lax.dot_general(
            xv[k], kgt[...], (((0,), (0,)), ((), ())), preferred_element_type=F32
        )
        for j in range(4):
            s_a[k, j] = block_of(k, 2, j).astype(BF16)
        remote(s_a.at[k, first], r_a.at[k, first], rs_send.at[0], a_recv.at[k, 0], up_y).start()
        remote(s_a.at[k, last], r_a.at[k, last], rs_send.at[0], a_recv.at[k, 1], down_y).start()

    def step_two(k):
        await_recv(r_a.at[k, first], a_recv.at[k, 0])
        for j in range(4):
            mine = block_of(k, 1, j)
            s_bp[k, j] = (mine + r_a[k, j].astype(F32) if j < 2 else mine).astype(BF16)
        remote(s_bp.at[k], r_bp.at[k], rs_send.at[1], b_recv.at[k, 0], up_y).start()
        await_recv(r_a.at[k, last], a_recv.at[k, 1])
        for j in range(4):
            mine = block_of(k, 3, j)
            s_bm[k, j] = (mine if j < 2 else mine + r_a[k, j].astype(F32)).astype(BF16)
        remote(s_bm.at[k], r_bm.at[k], rs_send.at[2], b_recv.at[k, 1], down_y).start()

    def split(block, place, send, key, same, flipped):
        for rows, slot, to in ((half, place, same[key]), (other, place + 1, flipped[key])):
            remote(block.at[rows], r_t.at[slot], send, t_recv.at[slot], to).start()

    def step_three(k):
        await_recv(r_bp.at[k], b_recv.at[k, 0])
        await_recv(r_bm.at[k], b_recv.at[k, 1])
        for j in (2, 1, 3, 0):
            summed = block_of(k, 0, j) + r_bp[k, j].astype(F32) + r_bm[k, j].astype(F32)
            if j == 0:
                own[k] = summed
                if k == 0:
                    s_o[...] = summed.astype(BF16)
                    remote(s_o.at[other], r_t.at[12], tail_send, t_recv.at[12], partner).start()
                continue
            s_z[k, j - 1] = summed.astype(BF16)
            if k == 0:
                split(s_z.at[0, j - 1], 2 * j - 2, rs_send.at[3], ZSTEP[j], near, near_flip)
            else:
                remote(
                    s_z.at[k, j - 1],
                    r_z.at[k, j - 1],
                    rs_send.at[3],
                    z_recv.at[k, j - 1],
                    near[ZSTEP[j]],
                ).start()

    def step_four(k):
        summed = own[k]
        for j in range(3):
            await_recv(r_z.at[k, j], z_recv.at[k, j])
            summed = summed + r_z[k, j].astype(F32)
        s_h[k] = summed.astype(BF16)
        split(s_h.at[k], 4 + 2 * k, rs_send.at[4], k, far, far_flip)

    inv[...] = jnp.zeros_like(inv)
    acc[...] = jnp.zeros_like(acc)
    for k in ORDER:
        await_recv(xv.at[k], sem_x.at[k])

        def squares(q, carry):
            for j in range(4):
                lanes = pl.ds(pl.multiple_of((q * 4 + j) * BLOCK, BLOCK), BLOCK)
                v = xv[k, :, lanes].astype(F32)
                inv[...] += v * v
            return carry

        lax.fori_loop(0, NY, squares, 0)
    scale = lax.rsqrt(jnp.sum(inv[...], axis=1, keepdims=True) * (1.0 / WIDTH) + NORM_EPS)
    inv[...] = jnp.broadcast_to(scale, inv.shape)
    loads[3].wait()
    kgt[...] = (kg[...].astype(F32) * inv[...]).astype(BF16)

    pl.semaphore_wait(barrier, len(peers))
    early_y()
    for k in (2, 1, 3):
        send_far(k)
    send_near(0)
    for k in range(1, NI):
        remote(
            diffs.at[isl], diffs.at[isl], d_send.at[k], d_recv.at[NI - k], islands[k - 1]
        ).start()

    for k in ORDER:
        step_one(k)
    send_y(0)
    early_z()
    wait_far(1)
    send_near(1)
    wait_far(3)
    send_near(3)
    step_two(2)
    wait_far(2)
    send_near(2)
    step_two(1)
    early_x(0)
    send_y(1)
    send_y(3)
    early_far(1)
    early_far(3)
    forward_y(0)
    send_y(2)
    early_far(2)
    step_two(3)
    early_x(1)
    early_x(3)
    early_x(2)
    forward_y(1)
    step_two(0)
    forward_y(3)
    step_three(2)
    opposite(0)
    step_three(1)
    forward_y(2)
    step_four(2)
    opposite(1)
    step_three(3)
    opposite(3)
    step_four(1)
    opposite(2)
    step_three(0)
    step_four(3)
    keys_part(0, 0)
    keys_part(0, 1)
    keys_part(0, 3)
    keys_part(1, 0)
    keys_part(3, 0)
    keys_part(2, 0)
    keys_part(1, 1)
    keys_part(1, 3)
    keys_part(3, 1)
    keys_part(3, 3)
    keys_part(0, 2)
    keys_part(2, 1)
    keys_part(2, 3)
    keys_part(1, 2)
    keys_part(3, 2)
    keys_part(2, 2)

    keys_out[...] = acc[...] * (inv[...] * WIDTH ** (-0.5))
    for k in range(1, NI):
        await_recv(diffs.at[(isl + k) % NI], d_recv.at[k])
    summed = diffs[0].astype(F32)
    for k in range(1, NI):
        summed = summed + diffs[k].astype(F32)
    drift_out[...] = summed * (1.0 / NI)

    await_recv(gw.at[pl.ds(1, 3), 0, 0, main], g_send.at[0])
    await_recv(gw.at[:, 0, pl.ds(1, 3), main], g_send.at[1])
    await_recv(gw.at[:, first, :, main], g_send.at[2])
    await_recv(gw.at[:, 2, :, main], g_send.at[3])
    await_recv(gw.at[:, :, :, half], g_send.at[4])
    await_recv(gw.at[0, pl.ds(1, 3), 0, early], g_send.at[5])
    await_recv(gw.at[pl.ds(1, 3), :, 0, early], g_send.at[6])
    await_recv(gw.at[:, :, pl.ds(1, 3), early], g_send.at[7])
    for k in range(1, NI):
        await_recv(diffs.at[0], d_send.at[k])
    await_recv(s_a, rs_send.at[0])
    await_recv(s_bp, rs_send.at[1])
    await_recv(s_bm, rs_send.at[2])
    await_recv(s_z, rs_send.at[3])
    await_recv(s_h.at[pl.ds(1, 3)], rs_send.at[4])
    await_recv(s_o.at[other], tail_send)

    summed = own[0, half, :]
    for slot in range(13):
        await_recv(r_t.at[slot], t_recv.at[slot])
        summed = summed + r_t[slot].astype(F32)
    usum_out[...] = summed


def adam_step(param, grad, first, second):
    first = BETA_ONE * first + (1.0 - BETA_ONE) * grad
    second = BETA_TWO * second + (1.0 - BETA_TWO) * grad * grad
    param = param - INNER_LR * (first / (jnp.sqrt(second) + ADAM_EPS) + DECAY * param)
    return (param, first, second)


def update(
    keys,
    unit_sum,
    drift,
    weight,
    weight_m,
    weight_v,
    gain,
    gain_m,
    gain_v,
    outer,
    momentum,
    fragment,
    active,
    keys_out,
    weight_out,
    weight_m_out,
    weight_v_out,
    gain_out,
    gain_m_out,
    gain_v_out,
    outer_out,
    momentum_out,
):
    key_scale = WIDTH ** (-0.5)
    eye = lax.broadcasted_iota(jnp.int32, (ROWS, ROWS), 0) == lax.broadcasted_iota(
        jnp.int32, (ROWS, ROWS), 1
    )

    def to_column(row):
        return jnp.sum(jnp.where(eye, row, jnp.zeros_like(row)), axis=1, keepdims=True)

    keys_out[...] = keys[...].astype(BF16)
    w, sums = weight[0], unit_sum[...]
    gain_bf = gain[...].astype(BF16).astype(F32)
    weight_grad = key_scale * to_column(gain_bf) * sums
    column = jnp.sum(w.astype(BF16).astype(F32) * sums, axis=1, keepdims=True)
    gain_grad = key_scale * jnp.sum(jnp.where(eye, column, 0.0), axis=0, keepdims=True)
    inner, first, second = adam_step(w, weight_grad, weight_m[0], weight_v[0])
    weight_m_out[0], weight_v_out[0] = first, second
    new, first, second = adam_step(gain[...], gain_grad, gain_m[...], gain_v[...])
    gain_out[...], gain_m_out[...], gain_v_out[...] = new, first, second
    pushed = OUTER_MU * momentum[...] + drift[...]
    candidate = outer[...] - OUTER_LR * (OUTER_MU * pushed + drift[...])
    current = lax.rem(active[...], NFRAG)
    chosen = jnp.where(fragment[...] == current, 1.0, 0.0)
    in_fragment = jnp.broadcast_to(to_column(chosen), (ROWS, HEAD)) > 0.5
    momentum_out[...] = jnp.where(in_fragment, pushed, momentum[...])
    outer_out[...] = jnp.where(in_fragment, candidate, outer[...])
    weight_out[0] = jnp.where(
        in_fragment, MIX_KEEP * inner + (1.0 - MIX_KEEP) * candidate, inner
    )


def shards(
    tokens,
    key_grad,
    weight,
    weight_m,
    weight_v,
    gain,
    gain_m,
    gain_v,
    outer,
    momentum,
    fragment_of_row,
    active_fragment,
):
    vmem = pl.BlockSpec(memory_space=pltpu.VMEM)
    block = (HEAD, BLOCK)
    dma = pltpu.SemaphoreType.DMA
    keys, unit_sum, outer_drift = pl.pallas_call(
        exchange,
        out_shape=(
            pltpu.VMEM((TOK, HEAD), F32),
            pltpu.VMEM((ROWS, HEAD), F32),
            pltpu.VMEM((ROWS, HEAD), F32),
        ),
        in_specs=[pl.BlockSpec(memory_space=pl.ANY)] * 5,
        out_specs=(vmem, vmem, vmem),
        scratch_shapes=[
            pltpu.VMEM((4, TOK, GROUP), BF16),
            pltpu.VMEM((4, NY, 4, BLOCK, HEAD), BF16),
            pltpu.VMEM((4, GROUP, HEAD), F32),
            *[pltpu.VMEM((4, 4) + block, BF16)] * 6,
            *[pltpu.VMEM((4, 3) + block, BF16)] * 2,
            pltpu.VMEM((4,) + block, BF16),
            pltpu.VMEM((4,) + block, F32),
            pltpu.VMEM(block, BF16),
            pltpu.VMEM((13, ROWS, HEAD), BF16),
            pltpu.VMEM((NI, ROWS, HEAD), BF16),
            pltpu.VMEM((TOK, HEAD), F32),
            pltpu.VMEM((TOK, HEAD), BF16),
            pltpu.VMEM((TOK, HEAD), F32),
            pltpu.VMEM((TOK, HEAD), BF16),
            pltpu.VMEM((1, ROWS, HEAD), F32),
            pltpu.VMEM((1, ROWS), F32),
            pltpu.VMEM((ROWS, HEAD), F32),
            dma((4,)),
            dma((4,)),
            dma((4,)),
            dma((4, 4)),
            dma((4, 4)),
            dma((4, 4)),
            dma((NY,)),
            dma((4,)),
            dma((4, 4)),
            dma((8,)),
            dma((4, 2)),
            dma((4, 2)),
            dma((4, 3)),
            dma((5,)),
            dma,
            dma((13,)),
            dma((NI,)),
            dma((NI,)),
        ],
        compiler_params=pltpu.CompilerParams(
            collective_id=0, has_side_effects=True, vmem_limit_bytes=60 * 2**20
        ),
        cost_estimate=pl.CostEstimate(
            flops=4 * TOK * WIDTH * HEAD, bytes_accessed=2 * TOK * WIDTH, transcendentals=0
        ),
    )(tokens, key_grad, weight, gain, outer)
    state = (ROWS, HEAD)
    results = pl.pallas_call(
        update,
        out_shape=(
            jax.ShapeDtypeStruct((TOK, HEAD), BF16),
            jax.ShapeDtypeStruct((1,) + state, F32),
            jax.ShapeDtypeStruct((1,) + state, F32),
            jax.ShapeDtypeStruct((1,) + state, F32),
            jax.ShapeDtypeStruct((1, ROWS), F32),
            jax.ShapeDtypeStruct((1, ROWS), F32),
            jax.ShapeDtypeStruct((1, ROWS), F32),
            jax.ShapeDtypeStruct(state, F32),
            jax.ShapeDtypeStruct(state, F32),
        ),
        in_specs=[vmem] * 13,
        out_specs=(vmem,) * 9,
        compiler_params=pltpu.CompilerParams(vmem_limit_bytes=4 * 2**20),
    )(
        keys,
        unit_sum,
        outer_drift,
        weight,
        weight_m,
        weight_v,
        gain,
        gain_m,
        gain_v,
        outer,
        momentum,
        fragment_of_row[None],
        active_fragment[None],
    )
    return results


def solution(mesh):
    return jax.shard_map(
        shards,
        mesh=mesh,
        in_specs=(
            P(("island", "fsdp"), None),
            P(("island", "fsdp"), None),
            P("island", "fsdp", None),
            P("island", "fsdp", None),
            P("island", "fsdp", None),
            P("island", "fsdp"),
            P("island", "fsdp"),
            P("island", "fsdp"),
            P("fsdp", None),
            P("fsdp", None),
            P("fsdp"),
            P(),
        ),
        out_specs=(
            P(("island", "fsdp"), None),
            P("island", "fsdp", None),
            P("island", "fsdp", None),
            P("island", "fsdp", None),
            P("island", "fsdp"),
            P("island", "fsdp"),
            P("island", "fsdp"),
            P("fsdp", None),
            P("fsdp", None),
        ),
        check_vma=False,
    )
```
